32 devices in a mesh: blk: 16 (over z, x, core), grp: 2 (over y).
Axes of the slice: x: 2, y: 2, z: 4, core: 2. Of those that a mesh axis runs over, the one named last changes fastest.
Arguments:
- activations: bfloat16 [8192, 8192], P('blk', 'grp'), may hold values from -6 to 6
- output_grads: bfloat16 [8192, 28672], P('blk', 'grp'), may hold values from -6 to 6
- query_left: bfloat16 [32, 32, 8192], P('blk', None, 'grp'), may hold values from -0.0078125 to 0.0078125
- query_right: bfloat16 [32, 32, 28672], P('blk', None, 'grp'), may hold values from -0.00390625 to 0.00390625
- basis_inputs: bfloat16 [16, 8192, 256], P('blk', 'grp'), may hold values from -0.0625 to 0.0625
- eigen_inputs: bfloat16 [16, 256], P('blk'), may hold values from 0.099609375 to 100
- basis_outputs: bfloat16 [16, 28672, 512], P('blk', 'grp'), may hold values from -0.03125 to 0.03125
- eigen_outputs: bfloat16 [16, 512], P('blk'), may hold values from 0.099609375 to 100
- owners: int32 [2], replicated, may hold values from 0 to 15
- seq_lengths: int32 [64], P('blk'), may hold values from 1 to 128, as said below
Outputs:
- scores: float32 [64, 32], P('blk')
The draws below stay inside these ranges and needn't reach their ends.
Inputs may be any that keep to these rules, and one draw needn't show every extreme that they name: `seq_lengths`: the 4 lengths of one shard sum to at most 512; in every draw some shard is full (all its lengths 128) and some sequence has length 1.
All inputs are finite; a program needn't handle non-finite values.
Results may differ from the reference program's by a relative error of at most 0.02.
Values may be sent and summed in bfloat16 or wider, within the bound.
A program may use at most 128 MiB of HBM per device.

```python
import math
import jax
import jax.numpy as jnp
from jax import lax

D = 8192
F = 28672
R = 32
KA = 256
KG = 512
TOK_DEV = 512
SEQ_DEV = 4
MAXLEN = 128
SHARDS = 16
QUERIES = 32
SEQS = 64
TOKENS = 8192
N_GRP = 2


def draw_seq_lengths(key, part):
    key_lens = jax.random.fold_in(key, 11)
    key_full = jax.random.fold_in(key, 12)
    key_other = jax.random.fold_in(key, 13)
    shard_count = SEQS // SEQ_DEV
    lengths = jax.random.randint(key_lens, (shard_count, SEQ_DEV), 1, MAXLEN + 1)
    full_row = jax.random.randint(key_full, (), 0, shard_count)
    other_row = (full_row + jax.random.randint(key_other, (), 1, shard_count)) % shard_count
    row_ids = jnp.arange(shard_count, dtype=jnp.int32)[:, None]
    col_ids = jnp.arange(SEQ_DEV, dtype=jnp.int32)[None, :]
    lengths = jnp.where(row_ids == full_row, MAXLEN, lengths)
    lengths = jnp.where((row_ids == other_row) & (col_ids == 0), 1, lengths)
    return lengths.reshape(-1).astype(jnp.int32)


def level_of(rng, shape, split, low, largest):
    level = 1.0
    for dim, parts in split:
        steps = jax.random.uniform(jax.random.fold_in(jax.random.fold_in(rng, 6), dim), (parts,), jnp.float32, low / len(split), largest / len(split))
        level = level * jnp.repeat(jnp.exp(steps), shape[dim] // parts).reshape((-1,) + (1,) * (len(shape) - 1 - dim))
    return level


def bell_draw(rng, shape, spread, limit, cuts=(), kind=jnp.bfloat16):
    result = jax.random.normal(rng, shape, jnp.float32) * spread
    if len(cuts) > 0:
        result = level_of(rng, shape, cuts, -0.22, 0.18) * result
    return jnp.clip(result, min=-limit, max=limit).astype(kind)


def setup_inputs(seed: int = 0) -> dict:
    splits = jax.random.split(jax.random.key(seed), 11)
    activations = bell_draw(splits[0], (TOKENS, D), 1.0, 6.0, ((0, 16), (1, 2)))
    output_grads = bell_draw(splits[1], (TOKENS, F), 1.0, 6.0, ((0, 16), (1, 2)))
    query_left = bell_draw(splits[2], (QUERIES, R, D), (64 * D) ** -0.5, 0.0078125, ((0, 16), (2, 2)))
    query_right = bell_draw(splits[3], (QUERIES, R, F), (64 * F) ** -0.5, 0.00390625, ((0, 16), (2, 2)))
    basis_inputs = bell_draw(splits[4], (SHARDS, D, KA), D ** -0.5, 0.0625, ((0, 16), (1, 2)))
    eigen_inputs = jnp.clip(jnp.exp(math.log(100.0) - 6.9116692 * jax.random.uniform(splits[5], (SHARDS, KA), jnp.float32) ** level_of(splits[5], (SHARDS, KA), ((0, 16),), -0.2, 0.2)), 0.099609375, 100.0).astype(jnp.bfloat16)
    basis_outputs = bell_draw(splits[6], (SHARDS, F, KG), F ** -0.5, 0.03125, ((0, 16), (1, 2)))
    eigen_outputs = jnp.clip(jnp.exp(math.log(100.0) - 6.9116692 * jax.random.uniform(splits[7], (SHARDS, KG), jnp.float32) ** level_of(splits[7], (SHARDS, KG), ((0, 16),), -0.2, 0.2)), 0.099609375, 100.0).astype(jnp.bfloat16)
    owners = jax.random.randint(splits[8], (2,), 0, SHARDS).astype(jnp.int32)
    seq_lengths = draw_seq_lengths(jax.random.fold_in(splits[10], 71), 0)
    return {"activations": activations, "output_grads": output_grads, "query_left": query_left, "query_right": query_right, "basis_inputs": basis_inputs, "eigen_inputs": eigen_inputs, "basis_outputs": basis_outputs, "eigen_outputs": eigen_outputs, "owners": owners, "seq_lengths": seq_lengths}


def contract(row_block, factors):
    return lax.dot_general(row_block, factors, (((1,), (1,)), ((), ())), preferred_element_type=jnp.float32)


def precondition(factors, basis, eigen):
    flat_rows = factors.reshape(-1, factors.shape[-1])
    coeffs = jnp.dot(flat_rows, basis, preferred_element_type=jnp.float32)
    eigen_float = eigen.astype(jnp.float32)
    damped = (coeffs * (eigen_float / (1.0 + eigen_float))).astype(jnp.bfloat16)
    return (flat_rows.astype(jnp.float32) - contract(damped, basis)).astype(jnp.bfloat16)


def project(row_block, factors):
    slot_count = row_block.shape[0]
    piece_width = row_block.shape[1] // N_GRP
    left_side = row_block.astype(jnp.float32).reshape(slot_count, N_GRP, piece_width)
    right_side = factors.astype(jnp.float32).reshape(factors.shape[0], N_GRP, piece_width)
    partial_value = jnp.einsum("tgd,qgd->gtq", left_side, right_side)
    rounded = lax.optimization_barrier(partial_value.astype(jnp.bfloat16))
    return jnp.sum(rounded.astype(jnp.float32), axis=0)


def membership(seq_lens):
    seq_ends = jnp.cumsum(seq_lens).astype(jnp.int32)
    seq_starts = seq_ends - seq_lens
    position = jnp.arange(TOK_DEV, dtype=jnp.int32)[None, :]
    inside = (position >= seq_starts[:, None]) & (position < seq_ends[:, None])
    return inside.astype(jnp.float32)


def reference(activations, output_grads, query_left, query_right, basis_inputs, eigen_inputs, basis_outputs, eigen_outputs, owners, seq_lengths):
    ready_left = precondition(query_left, basis_inputs[owners[0]], eigen_inputs[owners[0]])
    ready_right = precondition(query_right, basis_outputs[owners[1]], eigen_outputs[owners[1]])
    act_shards = activations.reshape(-1, TOK_DEV, D)
    grad_shards = output_grads.reshape(-1, TOK_DEV, F)
    length_rows = seq_lengths.reshape(-1, SEQ_DEV)

    def one_shard(shard_args):
        act_rows, grad_rows, seq_lens = shard_args
        proj_left = project(act_rows, ready_left)
        proj_right = project(grad_rows, ready_right)
        token_scores = jnp.sum((proj_left * proj_right).reshape(TOK_DEV, -1, R), axis=2)
        return jnp.dot(membership(seq_lens), token_scores, precision=lax.Precision.HIGHEST, preferred_element_type=jnp.float32)

    shard_scores = lax.map(one_shard, (act_shards, grad_shards, length_rows))
    return shard_scores.reshape(-1, QUERIES)
```

```python
import functools

import jax
import jax.numpy as jnp
from jax import lax
from jax.experimental import pallas as pl
from jax.experimental.pallas import tpu as pltpu
from jax.sharding import PartitionSpec as P

MESH = pl.DeviceIdType.MESH
HBM = pl.BlockSpec(memory_space=pltpu.HBM)


def broadcast(x, axis, root):
    mine = lax.axis_index(axis) == root
    return lax.psum(jnp.where(mine, x, jnp.zeros_like(x)), axis)


def contract(row_block, factors):
    return lax.dot_general(
        row_block, factors, (((1,), (1,)), ((), ())), preferred_element_type=jnp.float32
    )


def finish(flat_rows, coeffs, basis, eigen):
    eigen_float = eigen.astype(jnp.float32)
    damped = (coeffs * (eigen_float / (1.0 + eigen_float))).astype(jnp.bfloat16)
    return (flat_rows.astype(jnp.float32) - contract(damped, basis)).astype(jnp.bfloat16)


def membership(seq_lens, slot_count):
    seq_ends = jnp.cumsum(seq_lens)
    seq_starts = seq_ends - seq_lens
    position = jnp.arange(slot_count, dtype=jnp.int32)[None, :]
    inside = (position >= seq_starts[:, None]) & (position < seq_ends[:, None])
    return inside.astype(jnp.float32)


def grid_of(chips):
    cols = 1
    while cols * cols * 4 <= chips:
        cols *= 2
    return chips // cols, cols


def chip_at(place, chips):
    rows, cols = grid_of(chips)
    if cols == 1:
        return place
    wide = cols - 1
    row, step = place // wide, place % wide
    col = jnp.where(row % 2 == 0, 1 + step, wide - step)
    back = chips - 1 - place
    return jnp.where(place < rows * wide, row * cols + col, back * cols)


def place_of(chip, chips):
    rows, cols = grid_of(chips)
    if cols == 1:
        return chip
    wide = cols - 1
    row, col = chip // cols, chip % cols
    step = jnp.where(row % 2 == 0, col - 1, wide - col)
    return jnp.where(col == 0, chips - 1 - row, row * wide + step)


def wide_tile(width):
    tile = 2048
    while width % tile:
        tile //= 2
    return tile


def gather_kernel(
    chips,
    rows,
    act_ref,
    grad_ref,
    left_ref,
    right_ref,
    proj_left,
    proj_right,
    all_left,
    all_right,
    act,
    grad,
    block_left,
    block_right,
    total,
    load_sem,
    own_sem,
    ring_send,
    ring_recv,
    twin_send,
    twin_recv,
):
    me = lax.axis_index("blk")
    chip, core = me // 2, me % 2
    place = place_of(chip, chips)
    after = chip_at((place + 1) % chips, chips) * 2 + core
    before = chip_at((place + chips - 1) % chips, chips) * 2 + core
    twin = chip * 2 + 1 - core
    half = rows // 2
    mine = (left_ref, right_ref)
    gathered = (all_left, all_right)
    blocks = (block_left, block_right)

    barrier = pltpu.get_barrier_semaphore()
    for other in (after, before, twin):
        pl.semaphore_signal(barrier, inc=1, device_id={"blk": other}, device_id_type=MESH)
    pl.semaphore_wait(barrier, 3)

    def source(group, way):
        shift = (chips - group) if way == 0 else group
        return chip_at((place + shift) % chips, chips) * 2

    def ring_copy(group, way, part, src=None, arrived=0):
        ref = gathered[part].at[source(group + arrived, way) + core, pl.ds(way * half, half)]
        return pltpu.make_async_remote_copy(
            src_ref=ref if src is None else src,
            dst_ref=ref,
            send_sem=ring_send.at[group, way, part],
            recv_sem=ring_recv.at[group, way, part],
            device_id={"blk": after if way == 0 else before},
            device_id_type=MESH,
        )

    def twin_copy(group, way, part, src=None, side=core):
        ref = gathered[part].at[source(group, way) + side, pl.ds(way * half, half)]
        return pltpu.make_async_remote_copy(
            src_ref=ref if src is None else src,
            dst_ref=ref,
            send_sem=twin_send.at[group, way, part],
            recv_sem=twin_recv.at[group, way, part],
            device_id={"blk": twin},
            device_id_type=MESH,
        )

    own_copies = []
    for part in range(2):
        for way in range(2):
            piece = mine[part].at[pl.ds(way * half, half)]
            ring_copy(0, way, part, piece).start()
    for part in range(2):
        own_copies.append(
            pltpu.make_async_copy(mine[part], gathered[part].at[me], own_sem.at[part])
        )
        own_copies[-1].start()
        for way in range(2):
            piece = mine[part].at[pl.ds(way * half, half)]
            twin_copy(0, way, part, piece).start()
    own_copies.append(pltpu.make_async_copy(act_ref, act, own_sem.at[2]))
    own_copies[-1].start()
    own_copies.append(pltpu.make_async_copy(grad_ref, grad, own_sem.at[3]))
    own_copies[-1].start()
    for copy in own_copies:
        copy.wait()

    def step(group, carry):
        @pl.when(group < chips - 1)
        def _():
            for part in range(2):
                for way in range(2):
                    ring_copy(group, way, part, arrived=1).wait_recv()

                    @pl.when(group < chips - 2)
                    def _():
                        ring_copy(group + 1, way, part).start()

                    twin_copy(group + 1, way, part).start()

        loads = []
        for part in range(2):
            for way in range(2):
                twin_copy(group, way, part, side=1 - core).wait_recv()
                for side in range(2):
                    slot = way * 2 + side
                    load = pltpu.make_async_copy(
                        gathered[part].at[source(group, way) + side, pl.ds(way * half, half)],
                        blocks[part].at[pl.ds(slot * half, half)],
                        load_sem.at[slot, part],
                    )
                    load.start()
                    loads.append(load)
        for load in loads:
            load.wait()
        for part, (data, out) in enumerate(((act, proj_left), (grad, proj_right))):
            width = data.shape[1]
            tile = wide_tile(width)
            total[...] = jnp.zeros_like(total)

            @pl.loop(0, width // tile)
            def _(index):
                columns = pl.ds(pl.multiple_of(index * tile, tile), tile)
                total[...] += contract(blocks[part][:, columns], data[:, columns])

            for way in range(2):
                for side in range(2):
                    slot = way * 2 + side
                    start = (source(group, way) + side) * rows + way * half
                    out[pl.ds(pl.multiple_of(start, half), half), :] = total[
                        slot * half : (slot + 1) * half, :
                    ].astype(out.dtype)
        return carry

    lax.fori_loop(0, chips, step, 0)

    def drain(group, carry):
        for part in range(2):
            for way in range(2):
                @pl.when(group < chips - 1)
                def _():
                    ring_copy(group, way, part).wait_send()

                twin_copy(group, way, part).wait_send()
        return carry

    lax.fori_loop(0, chips, drain, 0)


def spread_kernel(chips, root, chunk, basis_ref, out_ref, own_sem, ring_send, ring_recv, twin_send, twin_recv):
    me = lax.axis_index("blk")
    chip, core = me // 2, me % 2
    place = place_of(chip, chips)
    after = chip_at((place + 1) % chips, chips) * 2 + core
    before = chip_at((place + chips - 1) % chips, chips) * 2 + core
    twin = chip * 2 + 1 - core
    hops = (place - place_of(root // 2, chips) + chips) % chips
    count = ring_send.shape[1]

    barrier = pltpu.get_barrier_semaphore()
    for other in (after, before, twin):
        pl.semaphore_signal(barrier, inc=1, device_id={"blk": other}, device_id_type=MESH)
    pl.semaphore_wait(barrier, 3)

    def rows_of(lane, way, index):
        start = ((lane * 2 + way) * count + index) * chunk
        return pl.ds(pl.multiple_of(start, chunk), chunk)

    def ring_copy(way, index, src=out_ref):
        rows = rows_of(core, way, index)
        return pltpu.make_async_remote_copy(
            src_ref=src.at[rows],
            dst_ref=out_ref.at[rows],
            send_sem=ring_send.at[way, index],
            recv_sem=ring_recv.at[way, index],
            device_id={"blk": after if way == 0 else before},
            device_id_type=MESH,
        )

    def twin_copy(lane, way, index, src=out_ref):
        rows = rows_of(lane, way, index)
        return pltpu.make_async_remote_copy(
            src_ref=src.at[rows],
            dst_ref=out_ref.at[rows],
            send_sem=twin_send.at[lane, way, index],
            recv_sem=twin_recv.at[lane, way, index],
            device_id={"blk": twin},
            device_id_type=MESH,
        )

    @pl.when(me == root)
    def _():
        own = pltpu.make_async_copy(basis_ref, out_ref, own_sem)

        @pl.loop(0, count)
        def _(index):
            for way in range(2):
                twin_copy(1 - core, way, index, basis_ref).start()
                ring_copy(way, index, basis_ref).start()

        own.start()

        @pl.loop(0, count)
        def _(index):
            for way in range(2):
                twin_copy(core, way, index, basis_ref).start()

        @pl.loop(0, count)
        def _(index):
            for way in range(2):
                twin_copy(1 - core, way, index, basis_ref).wait_send()
                ring_copy(way, index, basis_ref).wait_send()
                twin_copy(core, way, index, basis_ref).wait_send()

        own.wait()

    @pl.when((hops == 0) & (me != root))
    def _():
        @pl.loop(0, count)
        def _(index):
            for way in range(2):
                twin_copy(core, way, index).wait_recv()
                ring_copy(way, index).start()

        @pl.loop(0, count)
        def _(index):
            for way in range(2):
                twin_copy(1 - core, way, index).wait_recv()
                ring_copy(way, index).wait_send()

    @pl.when(hops > 0)
    def _():
        @pl.loop(0, count + chips)
        def _(tick):
            for way in range(2):
                gone = hops if way == 0 else chips - hops
                index = tick - gone

                @pl.when((index >= 0) & (index < count))
                def _():
                    ring_copy(way, index).wait_recv()

                    @pl.when(gone < chips - 1)
                    def _():
                        ring_copy(way, index).start()

                    twin_copy(core, way, index).start()

        @pl.loop(0, count)
        def _(index):
            for way in range(2):
                gone = hops if way == 0 else chips - hops
                twin_copy(1 - core, way, index).wait_recv()
                twin_copy(core, way, index).wait_send()

                @pl.when(gone < chips - 1)
                def _():
                    ring_copy(way, index).wait_send()


def spread(basis, size, root, first_id):
    quarter = basis.shape[0] // 4
    chunk = 128
    while quarter % chunk:
        chunk //= 2
    count = quarter // chunk
    return pl.pallas_call(
        functools.partial(spread_kernel, size // 2, root, chunk),
        out_shape=jax.ShapeDtypeStruct(basis.shape, basis.dtype),
        in_specs=[HBM],
        out_specs=HBM,
        scratch_shapes=[
            pltpu.SemaphoreType.DMA,
            pltpu.SemaphoreType.DMA((2, count)),
            pltpu.SemaphoreType.DMA((2, count)),
            pltpu.SemaphoreType.DMA((2, 2, count)),
            pltpu.SemaphoreType.DMA((2, 2, count)),
        ],
        compiler_params=pltpu.CompilerParams(
            collective_id=first_id + root, has_side_effects=True, vmem_limit_bytes=60 * 1024 * 1024
        ),
        cost_estimate=pl.CostEstimate(flops=0, bytes_accessed=2 * basis.size, transcendentals=0),
    )(basis)


def from_owner(basis, size, owner, first_id):
    branches = [
        functools.partial(spread, size=size, root=root, first_id=first_id) for root in range(size)
    ]
    return lax.switch(owner, branches, basis)


def gather_project(activations, output_grads, left, right, size):
    chips = size // 2
    rows = left.shape[0]
    slots = activations.shape[0]
    widths = (left.shape[1], right.shape[1])
    out = jax.ShapeDtypeStruct((size * rows, slots), jnp.bfloat16)
    vmem = pl.BlockSpec(memory_space=pltpu.VMEM)
    flops = 2 * size * rows * slots * sum(widths)
    return pl.pallas_call(
        functools.partial(gather_kernel, chips, rows),
        out_shape=[
            out,
            out,
            jax.ShapeDtypeStruct((size, rows, widths[0]), jnp.bfloat16),
            jax.ShapeDtypeStruct((size, rows, widths[1]), jnp.bfloat16),
        ],
        in_specs=[HBM] * 4,
        out_specs=[vmem, vmem, HBM, HBM],
        scratch_shapes=[
            pltpu.VMEM(activations.shape, jnp.bfloat16),
            pltpu.VMEM(output_grads.shape, jnp.bfloat16),
            pltpu.VMEM((2 * rows, widths[0]), jnp.bfloat16),
            pltpu.VMEM((2 * rows, widths[1]), jnp.bfloat16),
            pltpu.VMEM((2 * rows, slots), jnp.float32),
            pltpu.SemaphoreType.DMA((4, 2)),
            pltpu.SemaphoreType.DMA((4,)),
            pltpu.SemaphoreType.DMA((chips - 1, 2, 2)),
            pltpu.SemaphoreType.DMA((chips - 1, 2, 2)),
            pltpu.SemaphoreType.DMA((chips, 2, 2)),
            pltpu.SemaphoreType.DMA((chips, 2, 2)),
        ],
        compiler_params=pltpu.CompilerParams(
            collective_id=0, has_side_effects=True, vmem_limit_bytes=48 * 1024 * 1024
        ),
        cost_estimate=pl.CostEstimate(
            flops=flops, bytes_accessed=4 * size * rows * sum(widths), transcendentals=0
        ),
    )(activations, output_grads, left, right)[:2]


def make_local(mesh):
    size = mesh.shape["blk"]

    def local(
        activations,
        output_grads,
        query_left,
        query_right,
        basis_inputs,
        eigen_inputs,
        basis_outputs,
        eigen_outputs,
        owners,
        seq_lengths,
    ):
        basis_left, eigen_left = (
            from_owner(basis_inputs[0], size, owners[0], 1),
            broadcast(eigen_inputs[0], "blk", owners[0]),
        )
        basis_right, eigen_right = (
            from_owner(basis_outputs[0], size, owners[1], 1 + size),
            broadcast(eigen_outputs[0], "blk", owners[1]),
        )
        query_rank = query_left.shape[1]
        left_flat = query_left.reshape(-1, query_left.shape[2])
        right_flat = query_right.reshape(-1, query_right.shape[2])
        left_coeffs = jnp.dot(left_flat, basis_left, preferred_element_type=jnp.float32)
        right_coeffs = jnp.dot(right_flat, basis_right, preferred_element_type=jnp.float32)
        split = left_coeffs.shape[1]
        coeffs = jnp.concatenate([left_coeffs, right_coeffs], axis=1).astype(jnp.bfloat16)
        coeffs = lax.psum(coeffs, "grp").astype(jnp.float32)
        left_ready = finish(left_flat, coeffs[:, :split], basis_left, eigen_left)
        right_ready = finish(right_flat, coeffs[:, split:], basis_right, eigen_right)
        new_left, new_right = gather_project(
            activations, output_grads, left_ready, right_ready, size
        )
        slot_count = activations.shape[0]
        member = membership(seq_lengths, slot_count)
        both = jnp.stack([new_left, new_right])
        share = lax.psum_scatter(both, "grp", scatter_dimension=2, tiled=True)
        share = share.astype(jnp.float32)
        width = share.shape[2]
        product = (share[0] * share[1]).reshape(-1, query_rank, width)
        token_scores = jnp.sum(product, axis=1)
        member_part = lax.dynamic_slice_in_dim(
            member, lax.axis_index("grp") * width, width, 1
        )
        partial_scores = lax.dot_general(
            member_part,
            token_scores,
            (((1,), (1,)), ((), ())),
            precision=lax.Precision.HIGHEST,
            preferred_element_type=jnp.float32,
        )
        return lax.psum(partial_scores, "grp")

    return local


def solution(mesh):
    in_specs = (
        P("blk", "grp"),
        P("blk", "grp"),
        P("blk", None, "grp"),
        P("blk", None, "grp"),
        P("blk", "grp", None),
        P("blk", None),
        P("blk", "grp", None),
        P("blk", None),
        P(),
        P("blk"),
    )
    return jax.shard_map(
        make_local(mesh), mesh=mesh, in_specs=in_specs, out_specs=P("blk", None), check_vma=False
    )
```

```python
import functools

import jax
import jax.numpy as jnp
from jax import lax
from jax.experimental import pallas as pl
from jax.experimental.pallas import tpu as pltpu
from jax.sharding import PartitionSpec as P

MESH = pl.DeviceIdType.MESH
HBM = pl.BlockSpec(memory_space=pltpu.HBM)


def contract(row_block, factors):
    return lax.dot_general(
        row_block, factors, (((1,), (1,)), ((), ())), preferred_element_type=jnp.float32
    )


def finish(flat_rows, coeffs, basis, eigen):
    eigen_float = eigen.astype(jnp.float32)
    damped = (coeffs * (eigen_float / (1.0 + eigen_float))).astype(jnp.bfloat16)
    return (flat_rows.astype(jnp.float32) - contract(damped, basis)).astype(jnp.bfloat16)


def membership(seq_lens, slot_count):
    seq_ends = jnp.cumsum(seq_lens)
    seq_starts = seq_ends - seq_lens
    position = jnp.arange(slot_count, dtype=jnp.int32)[None, :]
    inside = (position >= seq_starts[:, None]) & (position < seq_ends[:, None])
    return inside.astype(jnp.float32)


def grid_of(chips):
    cols = 1
    while cols * cols * 4 <= chips:
        cols *= 2
    return chips // cols, cols


def chip_at(place, chips):
    rows, cols = grid_of(chips)
    if cols == 1:
        return place
    wide = cols - 1
    row, step = place // wide, place % wide
    col = jnp.where(row % 2 == 0, 1 + step, wide - step)
    back = chips - 1 - place
    return jnp.where(place < rows * wide, row * cols + col, back * cols)


def place_of(chip, chips):
    rows, cols = grid_of(chips)
    if cols == 1:
        return chip
    wide = cols - 1
    row, col = chip // cols, chip % cols
    step = jnp.where(row % 2 == 0, col - 1, wide - col)
    return jnp.where(col == 0, chips - 1 - row, row * wide + step)


def wide_tile(width):
    tile = 2048
    while width % tile:
        tile //= 2
    return tile


def gather_kernel(
    chips,
    rows,
    act_ref,
    grad_ref,
    left_ref,
    right_ref,
    proj_left,
    proj_right,
    all_left,
    all_right,
    act,
    grad,
    block_left,
    block_right,
    total,
    load_sem,
    own_sem,
    ring_send,
    ring_recv,
    twin_send,
    twin_recv,
):
    me = lax.axis_index("blk")
    chip, core = me // 2, me % 2
    place = place_of(chip, chips)
    after = chip_at((place + 1) % chips, chips) * 2 + core
    before = chip_at((place + chips - 1) % chips, chips) * 2 + core
    twin = chip * 2 + 1 - core
    half = rows // 2
    mine = (left_ref, right_ref)
    gathered = (all_left, all_right)
    blocks = (block_left, block_right)

    barrier = pltpu.get_barrier_semaphore()
    for other in (after, before, twin):
        pl.semaphore_signal(barrier, inc=1, device_id={"blk": other}, device_id_type=MESH)
    pl.semaphore_wait(barrier, 3)

    def source(group, way):
        shift = (chips - group) if way == 0 else group
        return chip_at((place + shift) % chips, chips) * 2

    def ring_copy(group, way, part, src=None, arrived=0):
        ref = gathered[part].at[source(group + arrived, way) + core, pl.ds(way * half, half)]
        return pltpu.make_async_remote_copy(
            src_ref=ref if src is None else src,
            dst_ref=ref,
            send_sem=ring_send.at[group, way, part],
            recv_sem=ring_recv.at[group, way, part],
            device_id={"blk": after if way == 0 else before},
            device_id_type=MESH,
        )

    def twin_copy(group, way, part, src=None, side=core):
        ref = gathered[part].at[source(group, way) + side, pl.ds(way * half, half)]
        return pltpu.make_async_remote_copy(
            src_ref=ref if src is None else src,
            dst_ref=ref,
            send_sem=twin_send.at[group, way, part],
            recv_sem=twin_recv.at[group, way, part],
            device_id={"blk": twin},
            device_id_type=MESH,
        )

    own_copies = []
    for part in range(2):
        for way in range(2):
            piece = mine[part].at[pl.ds(way * half, half)]
            ring_copy(0, way, part, piece).start()
    for part in range(2):
        own_rows = blocks[part].at[pl.ds(0, rows)]
        fetch = pltpu.make_async_copy(mine[part], own_rows, own_sem.at[part])
        fetch.start()
        fetch.wait()
        own_copies.append(
            pltpu.make_async_copy(own_rows, gathered[part].at[me], own_sem.at[part])
        )
        own_copies[-1].start()
        for way in range(2):
            piece = mine[part].at[pl.ds(way * half, half)]
            twin_copy(0, way, part, piece).start()
    own_copies.append(pltpu.make_async_copy(act_ref, act, own_sem.at[2]))
    own_copies[-1].start()
    own_copies.append(pltpu.make_async_copy(grad_ref, grad, own_sem.at[3]))
    own_copies[-1].start()
    for copy in own_copies:
        copy.wait()

    def step(group, carry):
        @pl.when(group < chips - 1)
        def _():
            for part in range(2):
                for way in range(2):
                    ring_copy(group, way, part, arrived=1).wait_recv()

                    @pl.when(group < chips - 2)
                    def _():
                        ring_copy(group + 1, way, part).start()

                    twin_copy(group + 1, way, part).start()

        loads = []
        for part in range(2):
            for way in range(2):
                twin_copy(group, way, part, side=1 - core).wait_recv()
                for side in range(2):
                    slot = way * 2 + side
                    load = pltpu.make_async_copy(
                        gathered[part].at[source(group, way) + side, pl.ds(way * half, half)],
                        blocks[part].at[pl.ds(slot * half, half)],
                        load_sem.at[slot, part],
                    )
                    load.start()
                    loads.append(load)
        for load in loads:
            load.wait()
        for part, (data, out) in enumerate(((act, proj_left), (grad, proj_right))):
            width = data.shape[1]
            tile = wide_tile(width)
            total[...] = jnp.zeros_like(total)

            @pl.loop(0, width // tile)
            def _(index):
                columns = pl.ds(pl.multiple_of(index * tile, tile), tile)
                total[...] += contract(blocks[part][:, columns], data[:, columns])

            for way in range(2):
                for side in range(2):
                    slot = way * 2 + side
                    start = (source(group, way) + side) * rows + way * half
                    out[pl.ds(pl.multiple_of(start, half), half), :] = total[
                        slot * half : (slot + 1) * half, :
                    ].astype(out.dtype)
        return carry

    lax.fori_loop(0, chips, step, 0)

    def drain(group, carry):
        for part in range(2):
            for way in range(2):
                @pl.when(group < chips - 1)
                def _():
                    ring_copy(group, way, part).wait_send()

                twin_copy(group, way, part).wait_send()
        return carry

    lax.fori_loop(0, chips, drain, 0)


def spread_kernel(chips, root, chunk, basis_ref, out_ref, stage, own_sem, ring_send, ring_recv, twin_send, twin_recv):
    me = lax.axis_index("blk")
    chip, core = me // 2, me % 2
    place = place_of(chip, chips)
    after = chip_at((place + 1) % chips, chips) * 2 + core
    before = chip_at((place + chips - 1) % chips, chips) * 2 + core
    twin = chip * 2 + 1 - core
    hops = (place - place_of(root // 2, chips) + chips) % chips
    count = ring_send.shape[1]

    barrier = pltpu.get_barrier_semaphore()
    for other in (after, before, twin):
        pl.semaphore_signal(barrier, inc=1, device_id={"blk": other}, device_id_type=MESH)
    pl.semaphore_wait(barrier, 3)

    def rows_of(lane, way, index):
        start = ((lane * 2 + way) * count + index) * chunk
        return pl.ds(pl.multiple_of(start, chunk), chunk)

    def ring_copy(way, index, src=out_ref):
        rows = rows_of(core, way, index)
        return pltpu.make_async_remote_copy(
            src_ref=src.at[rows],
            dst_ref=out_ref.at[rows],
            send_sem=ring_send.at[way, index],
            recv_sem=ring_recv.at[way, index],
            device_id={"blk": after if way == 0 else before},
            device_id_type=MESH,
        )

    def twin_copy(lane, way, index, src=out_ref):
        rows = rows_of(lane, way, index)
        return pltpu.make_async_remote_copy(
            src_ref=src.at[rows],
            dst_ref=out_ref.at[rows],
            send_sem=twin_send.at[lane, way, index],
            recv_sem=twin_recv.at[lane, way, index],
            device_id={"blk": twin},
            device_id_type=MESH,
        )

    @pl.when(me == root)
    def _():
        @pl.loop(0, count)
        def _(index):
            for way in range(2):
                twin_copy(1 - core, way, index, basis_ref).start()
                ring_copy(way, index, basis_ref).start()

        fetch = pltpu.make_async_copy(basis_ref, stage, own_sem.at[0])
        fetch.start()
        fetch.wait()
        store = pltpu.make_async_copy(stage, out_ref, own_sem.at[1])
        store.start()

        @pl.loop(0, count)
        def _(index):
            for way in range(2):
                twin_copy(core, way, index, basis_ref).start()

        @pl.loop(0, count)
        def _(index):
            for way in range(2):
                twin_copy(1 - core, way, index, basis_ref).wait_send()
                ring_copy(way, index, basis_ref).wait_send()
                twin_copy(core, way, index, basis_ref).wait_send()

        store.wait()

    @pl.when((hops == 0) & (me != root))
    def _():
        @pl.loop(0, count)
        def _(index):
            for way in range(2):
                twin_copy(core, way, index).wait_recv()
                ring_copy(way, index).start()

        @pl.loop(0, count)
        def _(index):
            for way in range(2):
                twin_copy(1 - core, way, index).wait_recv()
                ring_copy(way, index).wait_send()

    @pl.when(hops > 0)
    def _():
        @pl.loop(0, count + 2 * chips)
        def _(tick):
            for way in range(2):
                gone = hops if way == 0 else chips - hops
                index = tick - 2 * gone

                @pl.when((index >= 0) & (index < count))
                def _():
                    ring_copy(way, index).wait_recv()

                    @pl.when(gone < chips - 1)
                    def _():
                        ring_copy(way, index).start()

                    twin_copy(core, way, index).start()

        @pl.loop(0, count)
        def _(index):
            for way in range(2):
                gone = hops if way == 0 else chips - hops
                twin_copy(1 - core, way, index).wait_recv()
                twin_copy(core, way, index).wait_send()

                @pl.when(gone < chips - 1)
                def _():
                    ring_copy(way, index).wait_send()


def spread(basis, size, root, first_id):
    quarter = basis.shape[0] // 4
    chunk = 128
    while quarter % chunk:
        chunk //= 2
    count = quarter // chunk
    return pl.pallas_call(
        functools.partial(spread_kernel, size // 2, root, chunk),
        out_shape=jax.ShapeDtypeStruct(basis.shape, basis.dtype),
        in_specs=[HBM],
        out_specs=HBM,
        scratch_shapes=[
            pltpu.VMEM(basis.shape, basis.dtype),
            pltpu.SemaphoreType.DMA((2,)),
            pltpu.SemaphoreType.DMA((2, count)),
            pltpu.SemaphoreType.DMA((2, count)),
            pltpu.SemaphoreType.DMA((2, 2, count)),
            pltpu.SemaphoreType.DMA((2, 2, count)),
        ],
        compiler_params=pltpu.CompilerParams(
            collective_id=first_id + root, has_side_effects=True, vmem_limit_bytes=60 * 1024 * 1024
        ),
        cost_estimate=pl.CostEstimate(flops=0, bytes_accessed=2 * basis.size, transcendentals=0),
    )(basis)


def from_owner(basis, size, owner, first_id):
    branches = [
        functools.partial(spread, size=size, root=root, first_id=first_id) for root in range(size)
    ]
    return lax.switch(owner, branches, basis)


def exchange_sum(value, axis, count, width):
    me = lax.axis_index(axis)

    def part(index):
        if width is None:
            return value
        return lax.dynamic_slice_in_dim(value, index * width, width, value.ndim - 1)

    total = part(me).astype(jnp.float32)
    for shift in range(1, count):
        pairs = [(index, (index + shift) % count) for index in range(count)]
        total += lax.ppermute(part((me + shift) % count), axis, pairs).astype(jnp.float32)
    return total


def gather_project(activations, output_grads, left, right, size):
    chips = size // 2
    rows = left.shape[0]
    slots = activations.shape[0]
    widths = (left.shape[1], right.shape[1])
    out = jax.ShapeDtypeStruct((size * rows, slots), jnp.bfloat16)
    vmem = pl.BlockSpec(memory_space=pltpu.VMEM)
    flops = 2 * size * rows * slots * sum(widths)
    return pl.pallas_call(
        functools.partial(gather_kernel, chips, rows),
        out_shape=[
            out,
            out,
            jax.ShapeDtypeStruct((size, rows, widths[0]), jnp.bfloat16),
            jax.ShapeDtypeStruct((size, rows, widths[1]), jnp.bfloat16),
        ],
        in_specs=[HBM] * 4,
        out_specs=[vmem, vmem, HBM, HBM],
        scratch_shapes=[
            pltpu.VMEM(activations.shape, jnp.bfloat16),
            pltpu.VMEM(output_grads.shape, jnp.bfloat16),
            pltpu.VMEM((2 * rows, widths[0]), jnp.bfloat16),
            pltpu.VMEM((2 * rows, widths[1]), jnp.bfloat16),
            pltpu.VMEM((2 * rows, slots), jnp.float32),
            pltpu.SemaphoreType.DMA((4, 2)),
            pltpu.SemaphoreType.DMA((4,)),
            pltpu.SemaphoreType.DMA((chips - 1, 2, 2)),
            pltpu.SemaphoreType.DMA((chips - 1, 2, 2)),
            pltpu.SemaphoreType.DMA((chips, 2, 2)),
            pltpu.SemaphoreType.DMA((chips, 2, 2)),
        ],
        compiler_params=pltpu.CompilerParams(
            collective_id=0, has_side_effects=True, vmem_limit_bytes=48 * 1024 * 1024
        ),
        cost_estimate=pl.CostEstimate(
            flops=flops, bytes_accessed=4 * size * rows * sum(widths), transcendentals=0
        ),
    )(activations, output_grads, left, right)[:2]


def make_local(mesh):
    size = mesh.shape["blk"]
    groups = mesh.shape["grp"]

    def local(
        activations,
        output_grads,
        query_left,
        query_right,
        basis_inputs,
        eigen_inputs,
        basis_outputs,
        eigen_outputs,
        owners,
        seq_lengths,
    ):
        eigens = jnp.concatenate([eigen_inputs, eigen_outputs], axis=1)
        eigens = lax.all_gather(eigens, "blk", axis=0, tiled=True)
        split = eigen_inputs.shape[1]
        eigen_left = lax.dynamic_index_in_dim(eigens[:, :split], owners[0], 0, keepdims=False)
        eigen_right = lax.dynamic_index_in_dim(eigens[:, split:], owners[1], 0, keepdims=False)
        basis_left = from_owner(basis_inputs[0], size, owners[0], 1)
        basis_right = from_owner(basis_outputs[0], size, owners[1], 1 + size)
        query_rank = query_left.shape[1]
        left_flat = query_left.reshape(-1, query_left.shape[2])
        right_flat = query_right.reshape(-1, query_right.shape[2])
        left_coeffs = jnp.dot(left_flat, basis_left, preferred_element_type=jnp.float32)
        right_coeffs = jnp.dot(right_flat, basis_right, preferred_element_type=jnp.float32)
        coeffs = jnp.concatenate([left_coeffs, right_coeffs], axis=1).astype(jnp.bfloat16)
        coeffs = exchange_sum(coeffs, "grp", groups, None)
        left_ready = finish(left_flat, coeffs[:, :split], basis_left, eigen_left)
        right_ready = finish(right_flat, coeffs[:, split:], basis_right, eigen_right)
        new_left, new_right = gather_project(
            activations, output_grads, left_ready, right_ready, size
        )
        slot_count = activations.shape[0]
        member = membership(seq_lengths, slot_count)
        both = jnp.stack([new_left, new_right])
        width = slot_count // groups
        share = exchange_sum(both, "grp", groups, width)
        product = (share[0] * share[1]).reshape(-1, query_rank, width)
        token_scores = jnp.sum(product, axis=1)
        member_part = lax.dynamic_slice_in_dim(
            member, lax.axis_index("grp") * width, width, 1
        )
        partial_scores = lax.dot_general(
            member_part,
            token_scores,
            (((1,), (1,)), ((), ())),
            precision=lax.Precision.HIGHEST,
            preferred_element_type=jnp.float32,
        )
        return lax.psum(partial_scores, "grp")

    return local


def solution(mesh):
    in_specs = (
        P("blk", "grp"),
        P("blk", "grp"),
        P("blk", None, "grp"),
        P("blk", None, "grp"),
        P("blk", "grp", None),
        P("blk", None),
        P("blk", "grp", None),
        P("blk", None),
        P(),
        P("blk"),
    )
    return jax.shard_map(
        make_local(mesh), mesh=mesh, in_specs=in_specs, out_specs=P("blk", None), check_vma=False
    )
```
